512 devices in a mesh: seq: 32 (over x_hi, z), head: 4 (over y), dp: 4 (over x_lo, core).
Axes of the slice: x: 4 (x_hi: 2, x_lo: 2; x = x_hi * 2 + x_lo), y: 4, z: 16, core: 2. Of those that a mesh axis runs over, the one named last changes fastest.
Arguments:
- q_rows: bfloat16 [16384, 2560], P(('dp', 'seq'), 'head'), parts along dimension 0, may hold values from -6 to 6
- k_rows: bfloat16 [16384, 2560], P(('dp', 'seq'), 'head'), parts along dimension 0, may hold values from -6 to 6
- v_rows: bfloat16 [16384, 2560], P(('dp', 'seq'), 'head'), parts along dimension 0, may hold values from -6 to 6
- q_gain: float32 [2560], P('head'), may hold values from 0.8 to 2.5
- k_gain: float32 [2560], P('head'), may hold values from 0.8 to 2.5
- gate_table: float32 [50, 2560], P(None, 'head'), may hold values from 0.5 to 1.5
- clip_lengths: int32 [68], P('dp'), parts along dimension 0, may hold values from 1 to 512, 4096 in all
- clip_steps: int32 [68], P('dp'), parts along dimension 0, may hold values from 0 to 49
Outputs:
- attention_out: bfloat16 [16384, 2560], P(('dp', 'seq'), 'head'), parts along dimension 0
The draws below stay inside these ranges and needn't reach their ends.
There are 4 independent parts, one for each index of `dp`. The reference program is written for one: setup_inputs(seed, part) draws one part's arguments, and reference() takes and returns one part's arrays. A program takes and returns all parts, laid end to end along the dimension named above; an argument that names none is the same for every part. Nothing has to cross between parts.
Inputs may be any that keep to these rules, and one draw needn't show every extreme that they name: `clip_lengths`: the lengths sum to 4096; the longest clip has exactly 512 tokens.
All inputs are finite; a program needn't handle non-finite values.
Results may differ from the reference program's by a relative error of at most 0.011.
Values may be sent and summed in bfloat16 or wider, within the bound.
No kernel may reach another device: no remote copies, remote signals or barrier semaphores. Data moves between devices by JAX's collectives and lax.ppermute only.
A program may use at most 64 MiB of HBM per device.

```python
import math
import jax
import jax.numpy as jnp
import numpy as np
from jax import lax

TOK_DEV = 128
HEADS = 20
HD = 128
STEPS = 50
SPAN = 4
TOKENS = 4096
CLIPS = 17
CLIP_MOST = 512


def draw_q_rows(key, part):
    key = jax.random.fold_in(key, 11)
    base = jax.random.normal(key, (TOKENS, HEADS * HD), jnp.float32)
    return jnp.clip(base, -6.0, 6.0).astype(jnp.bfloat16)


def draw_k_rows(key, part):
    key = jax.random.fold_in(key, 12)
    base = jax.random.normal(key, (TOKENS, HEADS * HD), jnp.float32)
    return jnp.clip(base, -6.0, 6.0).astype(jnp.bfloat16)


def with_ends(values, rng, smallest, top_value):
    longest = values.shape.index(max(values.shape))
    spots = []
    for shift in (0, 1):
        where = [jax.random.randint(jax.random.fold_in(rng, axis), (), 0, length) for axis, length in enumerate(values.shape)]
        where[longest] = (where[longest] + shift) % values.shape[longest]
        spots.append(tuple(where))
    return values.at[spots[0]].set(smallest).at[spots[1]].set(top_value)


def steps_of(rng, shape, cuts, smallest, top_value):
    def one(dim, shards_of):
        draws = jax.random.uniform(jax.random.fold_in(jax.random.fold_in(rng, 6), dim), (shards_of,), jnp.float32, smallest / len(cuts), top_value / len(cuts))
        return jnp.repeat(jnp.exp(draws), shape[dim] // shards_of).reshape((-1,) + (1,) * (len(shape) - dim - 1))

    loudness = one(*cuts[0])
    for cut in cuts[1:]:
        loudness = loudness * one(*cut)
    return loudness


def length_profile(count, total, bound, lean):
    weights = [(1 << 20) // math.isqrt(rank ** lean) + 1 for rank in range(2, count + 1)]
    surplus, counts = total - bound - (count - 1), [1] * (count - 1)
    while surplus > 0:
        movable = [i for i in range(count - 1) if counts[i] < bound]
        whole, budget = sum([weights[i] for i in movable]), surplus
        for i in movable:
            addition = min(bound - counts[i], max(1, budget * weights[i] // whole), surplus)
            counts[i] = counts[i] + addition
            surplus = surplus - addition
    return np.array([bound] + counts)


def uneven(own_key, count, total, reach, skew):
    if count == 2:
        one = jax.random.randint(own_key, (), max(1, total - reach), min(reach, total - 1) + 1)
        return jnp.stack([one, total - one])
    lengths = jnp.asarray(length_profile(count, total, reach, skew), jnp.int32)
    twos = (count - 1) // 2
    donor, taker = lengths[1:1 + 2 * twos:2], lengths[2:2 + 2 * twos:2]
    room = jnp.minimum(donor - 1, reach - taker)
    passed = jax.random.randint(jax.random.fold_in(own_key, 1), (twos,), 0, 1 << 20) % (room + 1)
    lengths = lengths.at[1:1 + 2 * twos:2].set(donor - passed).at[2:2 + 2 * twos:2].set(taker + passed)
    return lengths[jax.random.permutation(jax.random.fold_in(own_key, 2), count)]


def scatter_about(stream_key, shape, deviation, limit, pieces=(), held_as=jnp.bfloat16):
    values = jax.random.normal(stream_key, shape, jnp.float32) * deviation
    if len(pieces) > 0:
        values = steps_of(stream_key, shape, pieces, -0.22, 0.18) * values
    return jnp.clip(values, min=-limit, max=limit).astype(held_as)


def setup_inputs(seed: int = 0, part: int = 0) -> dict:
    key_of = jax.random.split(jax.random.key(seed), 9)
    part_keys = jax.random.split(jax.random.fold_in(key_of[8], part), 9)
    q_rows = draw_q_rows(jax.random.fold_in(jax.random.fold_in(key_of[8], part), 71), part)
    k_rows = draw_k_rows(jax.random.fold_in(jax.random.fold_in(key_of[8], part), 71), part)
    v_rows = scatter_about(part_keys[2], (TOKENS, HEADS * HD), 1.0, 6.0, ((0, 32), (1, 4)))
    q_gain = jnp.clip(jnp.exp(math.log(2.5) - 1.13943427 * jax.random.uniform(key_of[3], (HEADS * HD,), jnp.float32) ** steps_of(key_of[3], (HEADS * HD,), ((0, 4),), -0.2, 0.2)), 0.8, 2.5)
    k_gain = jnp.clip(jnp.exp(math.log(2.5) - 1.13943427 * jax.random.uniform(key_of[4], (HEADS * HD,), jnp.float32) ** steps_of(key_of[4], (HEADS * HD,), ((0, 4),), -0.2, 0.2)), 0.8, 2.5)
    gate_table = jnp.clip(0.5 + 1.0 * jax.random.uniform(key_of[5], (STEPS, HEADS * HD), jnp.float32) ** steps_of(key_of[5], (STEPS, HEADS * HD), ((1, 4),), -0.2, 0.2), 0.5, 1.5)
    clip_lengths = uneven(part_keys[6], CLIPS, TOKENS, CLIP_MOST, 2).astype(jnp.int32)
    clip_steps = with_ends(jax.random.randint(part_keys[7], (CLIPS,), 0, STEPS), jax.random.fold_in(part_keys[7], 1), 0, STEPS - 1).astype(jnp.int32)
    return {"q_rows": q_rows, "k_rows": k_rows, "v_rows": v_rows, "q_gain": q_gain, "k_gain": k_gain, "gate_table": gate_table, "clip_lengths": clip_lengths, "clip_steps": clip_steps}


def clip_index(positions, ends):
    return lax.optimization_barrier(jnp.sum((positions[:, None] >= ends[None, :]).astype(jnp.int32), axis=1))

def rms_scale(rows, gain):
    data = rows.astype(jnp.float32)
    mean_square = lax.optimization_barrier(jnp.mean(data * data, axis=1, keepdims=True))
    return (data * lax.rsqrt(mean_square + 1e-06) * gain[None, :]).astype(jnp.bfloat16)

def reference(q_rows, k_rows, v_rows, q_gain, k_gain, gate_table, clip_lengths, clip_steps):
    ends = jnp.cumsum(clip_lengths).astype(jnp.int32)
    positions = jnp.arange(TOKENS, dtype=jnp.int32)
    row_clip = clip_index(positions, ends)
    gate_rows = gate_table[clip_steps[row_clip]]
    q_norm = rms_scale(q_rows, q_gain).reshape(TOKENS, HEADS, HD)
    k_norm = rms_scale(k_rows, k_gain).reshape(TOKENS, HEADS, HD)
    values = v_rows.reshape(TOKENS, HEADS, HD)
    window = min(TOKENS, (2 * SPAN + 1) * TOK_DEV)
    scale = HD ** (-0.5)

    def one_block(block):
        start = (block * TOK_DEV).astype(jnp.int32)
        low = jnp.clip(start - SPAN * TOK_DEV, 0, TOKENS - window).astype(jnp.int32)
        queries = lax.dynamic_slice_in_dim(q_norm, start, TOK_DEV, 0).astype(jnp.float32)
        keys = lax.dynamic_slice_in_dim(k_norm, low, window, 0).astype(jnp.float32)
        vals = lax.dynamic_slice_in_dim(values, low, window, 0).astype(jnp.float32)
        query_clip = lax.dynamic_slice_in_dim(row_clip, start, TOK_DEV, 0)
        key_clip = lax.dynamic_slice_in_dim(row_clip, low, window, 0)
        scores = jnp.einsum('qhd,khd->hqk', queries, keys) * scale
        mask = (query_clip[:, None] == key_clip[None, :])[None]
        scores = jnp.where(mask, scores, jnp.float32(-1e+30))
        highest = lax.optimization_barrier(jnp.max(scores, axis=-1))
        weights = jnp.where(mask, jnp.exp(scores - highest[..., None]), jnp.float32(0.0))
        total = lax.optimization_barrier(jnp.sum(weights, axis=-1))
        rounded = weights.astype(jnp.bfloat16).astype(jnp.float32)
        mixed = jnp.einsum('hqk,khd->qhd', rounded, vals)
        return mixed / jnp.transpose(total)[:, :, None]
    blocks = lax.map(one_block, jnp.arange(TOKENS // TOK_DEV, dtype=jnp.int32))
    mixed = blocks.reshape(TOKENS, HEADS * HD)
    return (gate_rows * mixed).astype(jnp.bfloat16)
```

```python
import functools
import math

import jax
import jax.numpy as jnp
from jax import lax
from jax.experimental import pallas as pl
from jax.experimental.pallas import tpu as pltpu
from jax.sharding import PartitionSpec as P

HEADS = 20
HD = 128
FAR = 3
LOW = -1e30
SCALE2 = HD ** (-0.5) * math.log2(math.e)
EXTRA = 16


def shifted(value, steps):
    count = lax.axis_size("seq")
    return lax.ppermute(value, "seq", [(source, (source + steps) % count) for source in range(count)])


def eye(size):
    return lax.broadcasted_iota(jnp.int32, (size, size), 0) == lax.broadcasted_iota(jnp.int32, (size, size), 1)


def as_row(column):
    size = column.shape[0]
    return jnp.sum(jnp.where(eye(size), column, 0.0), axis=0, keepdims=True)


def as_column(row):
    size = row.shape[1]
    return jnp.sum(jnp.where(eye(size), row, 0.0), axis=1, keepdims=True)


def clip_of(positions, lengths_ref):
    end = lengths_ref[0]
    found = (positions >= end).astype(jnp.int32)
    for clip in range(1, lengths_ref.shape[0]):
        end = end + lengths_ref[clip]
        found = found + (positions >= end).astype(jnp.int32)
    return found


def neighbour(place_ref, step):
    block, count = place_ref[0] + step, place_ref[1]
    return jnp.where(block < 0, block + count, jnp.where(block >= count, block - count, block))


def row_clips(block, rows, lengths_ref):
    return clip_of(block * rows + lax.broadcasted_iota(jnp.int32, (rows, 1), 0), lengths_ref)


def key_clips(block, rows, lengths_ref):
    return clip_of(block * rows + lax.broadcasted_iota(jnp.int32, (1, rows), 1), lengths_ref)


def squares_kernel(q_ref, k_ref, out_ref):
    def total(ref):
        data = ref[...].astype(jnp.float32)
        return as_row(jnp.sum(data * data, axis=1, keepdims=True))

    rows = out_ref.shape[2]
    both = jnp.concatenate([total(q_ref), total(k_ref), jnp.zeros((6, rows), jnp.float32)], axis=0)
    for peer in range(out_ref.shape[0]):
        out_ref[peer] = both


def norm_kernel(squares_ref, q_ref, k_ref, q_gain_ref, k_gain_ref, q_out, k_out):
    both = squares_ref[0]
    for peer in range(1, squares_ref.shape[0]):
        both = both + squares_ref[peer]
    factors = lax.rsqrt(both / (HEADS * HD) + 1e-06)
    for line, (ref, gain_ref, out) in enumerate([(q_ref, q_gain_ref, q_out), (k_ref, k_gain_ref, k_out)]):
        scaled = ref[...].astype(jnp.float32) * as_column(factors[line : line + 1])
        out[...] = (scaled * gain_ref[...]).astype(jnp.bfloat16)


def attend(queries, keys, values, masks):
    scores = [
        jnp.where(mask, lax.dot_general(queries, key, (((1,), (1,)), ((), ())), preferred_element_type=jnp.float32), LOW)
        for key, mask in zip(keys, masks)
    ]
    highest = jnp.max(functools.reduce(jnp.maximum, scores), axis=1, keepdims=True)
    weights = [jnp.exp2((score - highest) * SCALE2) for score in scores]
    total = jnp.sum(functools.reduce(jnp.add, weights), axis=1, keepdims=True)
    mixed = functools.reduce(
        jnp.add,
        [
            jnp.dot(weight.astype(jnp.bfloat16), value, preferred_element_type=jnp.float32)
            for weight, value in zip(weights, values)
        ],
    )
    return mixed / total, highest * SCALE2 + jnp.log2(total)


def guest_kernel(place_ref, lengths_ref, ql, qr, kl, km, kr, vl, vm, vr, left_out, right_out):
    rows, width = ql.shape
    key_ids = [key_clips(neighbour(place_ref, step), rows, lengths_ref) for step in (-FAR, 0, FAR)]
    for queries_ref, step, out in ((ql, -1, left_out), (qr, 1, right_out)):
        query_ids = row_clips(neighbour(place_ref, step), rows, lengths_ref)
        masks = [query_ids == ids for ids in key_ids]
        out[rows:, :] = jnp.zeros((EXTRA, width), jnp.bfloat16)
        for head in range(width // HD):
            at = slice(head * HD, (head + 1) * HD)
            mixed, level = attend(
                queries_ref[:, at], [ref[:, at] for ref in (kl, km, kr)], [ref[:, at] for ref in (vl, vm, vr)], masks
            )
            out[:rows, at] = mixed.astype(jnp.bfloat16)
            rest = as_row(level)
            lines = []
            for _ in range(3):
                piece = rest.astype(jnp.bfloat16)
                rest = rest - piece.astype(jnp.float32)
                lines.append(piece.astype(jnp.float32))
            pad = jnp.zeros((EXTRA - 3, rows), jnp.float32)
            out[rows:, at] = jnp.concatenate(lines + [pad], axis=0).astype(jnp.bfloat16)


def home_kernel(place_ref, lengths_ref, steps_ref, table, q, kl, km, kr, vl, vm, vr, mixed_out, level_out, gate_out):
    rows, width = q.shape
    query_ids = row_clips(place_ref[0], rows, lengths_ref)
    masks = [query_ids == key_clips(neighbour(place_ref, step), rows, lengths_ref) for step in (-FAR, 0, FAR)]
    levels = []
    for head in range(width // HD):
        at = slice(head * HD, (head + 1) * HD)
        mixed, level = attend(q[:, at], [ref[:, at] for ref in (kl, km, kr)], [ref[:, at] for ref in (vl, vm, vr)], masks)
        mixed_out[:, at] = mixed
        levels.append(jnp.broadcast_to(level, (rows, HD)))
    for head, level in enumerate(levels):
        level_out[:, head * HD : (head + 1) * HD] = level
    gate = jnp.zeros((rows, width), jnp.float32)
    for clip in range(lengths_ref.shape[0]):
        gate = jnp.where(query_ids == clip, table[pl.ds(steps_ref[clip], 1), :], gate)
    gate_out[...] = gate


def join_kernel(gate, mixed, levels, from_left, from_right, out):
    rows, width = mixed.shape
    for head in range(width // HD):
        at = slice(head * HD, (head + 1) * HD)
        parts = [(levels[:, at], mixed[:, at])]
        for ref in (from_left, from_right):
            lines = ref[rows:, at].astype(jnp.float32)
            level = as_column(lines[0:1] + lines[1:2] + lines[2:3])
            parts.append((level, ref[:rows, at].astype(jnp.float32)))
        top = functools.reduce(jnp.maximum, [level for level, _ in parts])
        shares = [jnp.exp2(level - top) for level, _ in parts]
        total = functools.reduce(jnp.add, shares)
        joined = functools.reduce(jnp.add, [share * part for share, (_, part) in zip(shares, parts)])
        out[:, at] = (gate[:, at] * joined / total).astype(jnp.bfloat16)


def call(kernel, outs, scalars, arrays, flops=0):
    space = [pl.BlockSpec(memory_space=pltpu.SMEM)] * len(scalars) + [pl.BlockSpec(memory_space=pltpu.VMEM)] * len(arrays)
    size = sum(math.prod(a.shape) * a.dtype.itemsize for a in list(arrays) + list(outs))
    return pl.pallas_call(
        kernel,
        out_shape=outs,
        in_specs=space,
        out_specs=[pl.BlockSpec(memory_space=pltpu.VMEM)] * len(outs),
        compiler_params=pltpu.CompilerParams(vmem_limit_bytes=32 * 2**20),
        cost_estimate=pl.CostEstimate(flops=flops, bytes_accessed=size, transcendentals=0),
    )(*scalars, *arrays)


def per_device(q_rows, k_rows, v_rows, q_gain, k_gain, gate_table, clip_lengths, clip_steps):
    rows, width = q_rows.shape
    heads_here = width // HD
    peers = lax.axis_size("head")
    place = jnp.stack([lax.axis_index("seq"), lax.axis_size("seq")]).astype(jnp.int32)
    bf16 = functools.partial(jax.ShapeDtypeStruct, dtype=jnp.bfloat16)
    f32 = functools.partial(jax.ShapeDtypeStruct, dtype=jnp.float32)

    v_left, v_right = shifted(v_rows, FAR), shifted(v_rows, -FAR)
    (squares,) = call(squares_kernel, [f32((peers, 8, rows))], [], [q_rows, k_rows])
    squares = lax.all_to_all(squares, "head", 0, 0)
    q_norm, k_norm = call(
        norm_kernel,
        [bf16((rows, width)), bf16((rows, width))],
        [],
        [squares, q_rows, k_rows, q_gain.reshape(1, width), k_gain.reshape(1, width)],
    )
    k_left, k_right = shifted(k_norm, FAR), shifted(k_norm, -FAR)
    q_left, q_right = shifted(q_norm, 1), shifted(q_norm, -1)
    around = [k_left, k_norm, k_right, v_left, v_rows, v_right]
    flops = 4 * rows * 3 * rows * HD * heads_here
    to_left, to_right = call(
        guest_kernel,
        [bf16((rows + EXTRA, width))] * 2,
        [place, clip_lengths],
        [q_left, q_right] + around,
        2 * flops,
    )
    from_right, from_left = shifted(to_left, -1), shifted(to_right, 1)
    mixed, levels, gate = call(
        home_kernel,
        [f32((rows, width))] * 3,
        [place, clip_lengths, clip_steps],
        [gate_table, q_norm] + around,
        flops,
    )
    (out,) = call(
        join_kernel, [bf16((rows, width))], [], [gate, mixed, levels, from_left, from_right]
    )
    return out


def solution(mesh):
    placed = (
        P(("dp", "seq"), "head"),
        P(("dp", "seq"), "head"),
        P(("dp", "seq"), "head"),
        P("head"),
        P("head"),
        P(None, "head"),
        P("dp"),
        P("dp"),
    )
    return jax.shard_map(
        per_device, mesh=mesh, in_specs=placed, out_specs=P(("dp", "seq"), "head"), check_vma=False
    )
```

```python
import functools
import math

import jax
import jax.numpy as jnp
from jax import lax
from jax.experimental import pallas as pl
from jax.experimental.pallas import tpu as pltpu
from jax.sharding import PartitionSpec as P

HEADS = 20
HD = 128
FAR = 3
LOW = -1e30
SCALE2 = HD ** (-0.5) * math.log2(math.e)
EXTRA = 16


def hop(value, steps):
    count, parts = lax.axis_size("seq"), lax.axis_size("dp")
    pairs = []
    for source in range(count):
        for part in range(parts):
            target = source + (steps if part % 2 == 0 else -steps)
            if 0 <= target < count or (source, target % count) in ((2, count - 1), (count - FAR, 0)) or abs(steps) == 1:
                pairs.append((source * parts + part, target % count * parts + part))
    return lax.ppermute(value, ("seq", "dp"), pairs)


def eye(size):
    return lax.broadcasted_iota(jnp.int32, (size, size), 0) == lax.broadcasted_iota(jnp.int32, (size, size), 1)


def as_row(column):
    size = column.shape[0]
    return jnp.sum(jnp.where(eye(size), column, 0.0), axis=0, keepdims=True)


def as_column(row):
    size = row.shape[1]
    return jnp.sum(jnp.where(eye(size), row, 0.0), axis=1, keepdims=True)


def clip_of(positions, lengths_ref):
    end = lengths_ref[0]
    found = (positions >= end).astype(jnp.int32)
    for clip in range(1, lengths_ref.shape[0]):
        end = end + lengths_ref[clip]
        found = found + (positions >= end).astype(jnp.int32)
    return found


def neighbour(place_ref, step):
    block, count = place_ref[0] + step * place_ref[2], place_ref[1]
    return jnp.where(block < 0, block + count, jnp.where(block >= count, block - count, block))


def row_clips(block, rows, lengths_ref):
    return clip_of(block * rows + lax.broadcasted_iota(jnp.int32, (rows, 1), 0), lengths_ref)


def key_clips(block, rows, lengths_ref):
    return clip_of(block * rows + lax.broadcasted_iota(jnp.int32, (1, rows), 1), lengths_ref)


def squares_kernel(q_ref, k_ref, out_ref):
    def total(ref):
        data = ref[...].astype(jnp.float32)
        return as_row(jnp.sum(data * data, axis=1, keepdims=True))

    rows = out_ref.shape[2]
    both = jnp.concatenate([total(q_ref), total(k_ref), jnp.zeros((6, rows), jnp.float32)], axis=0)
    for peer in range(out_ref.shape[0]):
        out_ref[peer] = both


def norm_kernel(squares_ref, q_ref, k_ref, q_gain_ref, k_gain_ref, q_out, k_out):
    both = squares_ref[0]
    for peer in range(1, squares_ref.shape[0]):
        both = both + squares_ref[peer]
    factors = lax.rsqrt(both / (HEADS * HD) + 1e-06)
    for line, (ref, gain_ref, out) in enumerate([(q_ref, q_gain_ref, q_out), (k_ref, k_gain_ref, k_out)]):
        scaled = ref[...].astype(jnp.float32) * as_column(factors[line : line + 1])
        out[...] = (scaled * gain_ref[...]).astype(jnp.bfloat16)


def attend(queries, keys, values, masks):
    heads = range(queries.shape[1] // HD)
    at = [slice(head * HD, (head + 1) * HD) for head in heads]
    scores = [
        [
            jnp.where(
                mask,
                lax.dot_general(
                    queries[:, at[h]], key[:, at[h]], (((1,), (1,)), ((), ())), preferred_element_type=jnp.float32
                ),
                LOW,
            )
            for key, mask in zip(keys, masks)
        ]
        for h in heads
    ]
    highest = [jnp.max(functools.reduce(jnp.maximum, scores[h]), axis=1, keepdims=True) for h in heads]
    weights = [[jnp.exp2((score - highest[h]) * SCALE2) for score in scores[h]] for h in heads]
    total = [jnp.sum(functools.reduce(jnp.add, weights[h]), axis=1, keepdims=True) for h in heads]
    mixed = [
        functools.reduce(
            jnp.add,
            [
                jnp.dot(weight.astype(jnp.bfloat16), value[:, at[h]], preferred_element_type=jnp.float32)
                for weight, value in zip(weights[h], values)
            ],
        )
        for h in heads
    ]
    return [(at[h], mixed[h] / total[h], highest[h] * SCALE2 + jnp.log2(total[h])) for h in heads]


def guest_kernel(step, place_ref, lengths_ref, queries, kl, km, kr, vl, vm, vr, out):
    rows, width = queries.shape
    query_ids = row_clips(neighbour(place_ref, step), rows, lengths_ref)
    masks = [query_ids == key_clips(neighbour(place_ref, far), rows, lengths_ref) for far in (-FAR, 0, FAR)]
    for at, mixed, level in attend(queries, (kl, km, kr), (vl, vm, vr), masks):
        out[:rows, at] = mixed.astype(jnp.bfloat16)
        rest = as_row(level)
        lines = []
        for _ in range(3):
            piece = rest.astype(jnp.bfloat16)
            rest = rest - piece.astype(jnp.float32)
            lines.append(piece.astype(jnp.float32))
        pad = jnp.zeros((EXTRA - 3, rows), jnp.float32)
        out[rows:, at] = jnp.concatenate(lines + [pad], axis=0).astype(jnp.bfloat16)


def home_kernel(place_ref, lengths_ref, steps_ref, table, q, kl, km, kr, vl, vm, vr, mixed_out, level_out, gate_out):
    rows, width = q.shape
    query_ids = row_clips(place_ref[0], rows, lengths_ref)
    masks = [query_ids == key_clips(neighbour(place_ref, far), rows, lengths_ref) for far in (-FAR, 0, FAR)]
    for at, mixed, level in attend(q, (kl, km, kr), (vl, vm, vr), masks):
        mixed_out[:, at] = mixed
        level_out[:, at] = jnp.broadcast_to(level, (rows, HD))
    gate = jnp.zeros((rows, width), jnp.float32)
    for clip in range(lengths_ref.shape[0]):
        gate = jnp.where(query_ids == clip, table[pl.ds(steps_ref[clip], 1), :], gate)
    gate_out[...] = gate


def join_kernel(gate, mixed, levels, from_left, from_right, out):
    rows, width = mixed.shape
    for head in range(width // HD):
        at = slice(head * HD, (head + 1) * HD)
        parts = [(levels[:, at], mixed[:, at])]
        for ref in (from_left, from_right):
            lines = ref[rows:, at].astype(jnp.float32)
            level = as_column(lines[0:1] + lines[1:2] + lines[2:3])
            parts.append((level, ref[:rows, at].astype(jnp.float32)))
        top = functools.reduce(jnp.maximum, [level for level, _ in parts])
        shares = [jnp.exp2(level - top) for level, _ in parts]
        total = functools.reduce(jnp.add, shares)
        joined = functools.reduce(jnp.add, [share * part for share, (_, part) in zip(shares, parts)])
        out[:, at] = (gate[:, at] * joined / total).astype(jnp.bfloat16)


def call(kernel, outs, scalars, arrays, flops=0):
    space = [pl.BlockSpec(memory_space=pltpu.SMEM)] * len(scalars) + [pl.BlockSpec(memory_space=pltpu.VMEM)] * len(arrays)
    size = sum(math.prod(a.shape) * a.dtype.itemsize for a in list(arrays) + list(outs))
    return pl.pallas_call(
        kernel,
        out_shape=outs,
        in_specs=space,
        out_specs=[pl.BlockSpec(memory_space=pltpu.VMEM)] * len(outs),
        compiler_params=pltpu.CompilerParams(vmem_limit_bytes=32 * 2**20),
        cost_estimate=pl.CostEstimate(flops=flops, bytes_accessed=size, transcendentals=0),
    )(*scalars, *arrays)


def per_device(q_rows, k_rows, v_rows, q_gain, k_gain, gate_table, clip_lengths, clip_steps):
    rows, width = q_rows.shape
    heads_here = width // HD
    peers = lax.axis_size("head")
    turn = 1 - 2 * (lax.axis_index("dp") % 2)
    place = jnp.stack([lax.axis_index("seq"), lax.axis_size("seq"), turn]).astype(jnp.int32)
    bf16 = functools.partial(jax.ShapeDtypeStruct, dtype=jnp.bfloat16)
    f32 = functools.partial(jax.ShapeDtypeStruct, dtype=jnp.float32)

    v_near, v_next = hop(v_rows, FAR), hop(v_rows, -FAR)
    (squares,) = call(squares_kernel, [f32((peers, 8, rows))], [], [q_rows, k_rows])
    squares = lax.all_to_all(squares, "head", 0, 0)
    q_norm, k_norm = call(
        norm_kernel,
        [bf16((rows, width)), bf16((rows, width))],
        [],
        [squares, q_rows, k_rows, q_gain.reshape(1, width), k_gain.reshape(1, width)],
    )
    k_near, k_next = hop(k_norm, FAR), hop(k_norm, -FAR)
    q_near, q_next = hop(q_norm, 1), hop(q_norm, -1)
    around = [k_near, k_norm, k_next, v_near, v_rows, v_next]
    flops = 4 * rows * 3 * rows * HD * heads_here
    returned = []
    for queries, step in ((q_near, -1), (q_next, 1)):
        (partial,) = call(
            functools.partial(guest_kernel, step),
            [bf16((rows + EXTRA, width))],
            [place, clip_lengths],
            [queries] + around,
            flops,
        )
        returned.append(hop(partial, step))
    from_right, from_left = returned
    mixed, levels, gate = call(
        home_kernel,
        [f32((rows, width))] * 3,
        [place, clip_lengths, clip_steps],
        [gate_table, q_norm] + around,
        flops,
    )
    (out,) = call(
        join_kernel, [bf16((rows, width))], [], [gate, mixed, levels, from_left, from_right]
    )
    return out


def solution(mesh):
    placed = (
        P(("dp", "seq"), "head"),
        P(("dp", "seq"), "head"),
        P(("dp", "seq"), "head"),
        P("head"),
        P("head"),
        P(None, "head"),
        P("dp"),
        P("dp"),
    )
    return jax.shard_map(
        per_device, mesh=mesh, in_specs=placed, out_specs=P(("dp", "seq"), "head"), check_vma=False
    )
```

```python
import functools
import math

import jax
import jax.numpy as jnp
from jax import lax
from jax.experimental import pallas as pl
from jax.experimental.pallas import tpu as pltpu
from jax.sharding import PartitionSpec as P

HEADS = 20
HD = 128
FAR = 3
LOW = -1e30
SCALE2 = HD ** (-0.5) * math.log2(math.e)
EXTRA = 16


def hop(value, steps):
    count, parts = lax.axis_size("seq"), lax.axis_size("dp")
    pairs = []
    for source in range(count):
        for part in range(parts):
            target = source + (steps if part % 2 == 0 else -steps)
            if 0 <= target < count or (source, target % count) in ((2, count - 1), (count - FAR, 0)) or abs(steps) == 1:
                pairs.append((source * parts + part, target % count * parts + part))
    return lax.ppermute(value, ("seq", "dp"), pairs)


def eye(size):
    return lax.broadcasted_iota(jnp.int32, (size, size), 0) == lax.broadcasted_iota(jnp.int32, (size, size), 1)


def as_row(column):
    size = column.shape[0]
    return jnp.sum(jnp.where(eye(size), column, 0.0), axis=0, keepdims=True)


def as_column(row):
    size = row.shape[1]
    return jnp.sum(jnp.where(eye(size), row, 0.0), axis=1, keepdims=True)


def clip_of(positions, lengths_ref):
    end = lengths_ref[0]
    found = (positions >= end).astype(jnp.int32)
    for clip in range(1, lengths_ref.shape[0]):
        end = end + lengths_ref[clip]
        found = found + (positions >= end).astype(jnp.int32)
    return found


def neighbour(place_ref, step):
    block, count = place_ref[0] + step * place_ref[2], place_ref[1]
    return jnp.where(block < 0, block + count, jnp.where(block >= count, block - count, block))


def row_clips(block, rows, lengths_ref):
    return clip_of(block * rows + lax.broadcasted_iota(jnp.int32, (rows, 1), 0), lengths_ref)


def key_clips(block, rows, lengths_ref):
    return clip_of(block * rows + lax.broadcasted_iota(jnp.int32, (1, rows), 1), lengths_ref)


def squares_kernel(both_ref, out_ref):
    rows = out_ref.shape[2]
    lines = []
    for index in range(2):
        data = both_ref[index].astype(jnp.float32)
        lines.append(as_row(jnp.sum(data * data, axis=1, keepdims=True)))
    lines = jnp.concatenate(lines + [jnp.zeros((6, rows), jnp.float32)], axis=0)
    for peer in range(out_ref.shape[0]):
        out_ref[peer] = lines


def norm_kernel(index, squares_ref, both_ref, gain_ref, *rest):
    total = squares_ref[0]
    for peer in range(1, squares_ref.shape[0]):
        total = total + squares_ref[peer]
    factors = lax.rsqrt(total / (HEADS * HD) + 1e-06)
    scaled = both_ref[index].astype(jnp.float32) * as_column(factors[index : index + 1])
    rest[-1][...] = (scaled * gain_ref[...]).astype(jnp.bfloat16)


def attend(queries, keys, values, masks):
    heads = range(queries.shape[1] // HD)
    at = [slice(head * HD, (head + 1) * HD) for head in heads]
    scores = [
        [
            jnp.where(
                mask,
                lax.dot_general(
                    queries[:, at[h]], key[:, at[h]], (((1,), (1,)), ((), ())), preferred_element_type=jnp.float32
                ),
                LOW,
            )
            for key, mask in zip(keys, masks)
        ]
        for h in heads
    ]
    highest = [jnp.max(functools.reduce(jnp.maximum, scores[h]), axis=1, keepdims=True) for h in heads]
    weights = [[jnp.exp2((score - highest[h]) * SCALE2) for score in scores[h]] for h in heads]
    total = [jnp.sum(functools.reduce(jnp.add, weights[h]), axis=1, keepdims=True) for h in heads]
    mixed = [
        functools.reduce(
            jnp.add,
            [
                jnp.dot(weight.astype(jnp.bfloat16), value[:, at[h]], preferred_element_type=jnp.float32)
                for weight, value in zip(weights[h], values)
            ],
        )
        for h in heads
    ]
    return [(at[h], mixed[h] / total[h], highest[h] * SCALE2 + jnp.log2(total[h])) for h in heads]


def guest_kernel(step, place_ref, lengths_ref, queries, kl, km, kr, vl, vm, vr, out):
    rows, width = queries.shape
    query_ids = row_clips(neighbour(place_ref, step), rows, lengths_ref)
    masks = [query_ids == key_clips(neighbour(place_ref, far), rows, lengths_ref) for far in (-FAR, 0, FAR)]
    for at, mixed, level in attend(queries, (kl, km, kr), (vl, vm, vr), masks):
        out[:rows, at] = mixed.astype(jnp.bfloat16)
        rest = as_row(level)
        lines = []
        for _ in range(3):
            piece = rest.astype(jnp.bfloat16)
            rest = rest - piece.astype(jnp.float32)
            lines.append(piece.astype(jnp.float32))
        pad = jnp.zeros((EXTRA - 3, rows), jnp.float32)
        out[rows:, at] = jnp.concatenate(lines + [pad], axis=0).astype(jnp.bfloat16)


def home_kernel(place_ref, lengths_ref, steps_ref, table, q, kl, km, kr, vl, vm, vr, mixed_out, level_out, gate_out):
    rows, width = q.shape
    query_ids = row_clips(place_ref[0], rows, lengths_ref)
    masks = [query_ids == key_clips(neighbour(place_ref, far), rows, lengths_ref) for far in (-FAR, 0, FAR)]
    for at, mixed, level in attend(q, (kl, km, kr), (vl, vm, vr), masks):
        mixed_out[:, at] = mixed
        level_out[:, at] = jnp.broadcast_to(level, (rows, HD))
    gate = jnp.zeros((rows, width), jnp.float32)
    for clip in range(lengths_ref.shape[0]):
        gate = jnp.where(query_ids == clip, table[pl.ds(steps_ref[clip], 1), :], gate)
    gate_out[...] = gate


def join_kernel(gate, mixed, levels, from_left, from_right, out):
    rows, width = mixed.shape
    for head in range(width // HD):
        at = slice(head * HD, (head + 1) * HD)
        parts = [(levels[:, at], mixed[:, at])]
        for ref in (from_left, from_right):
            lines = ref[rows:, at].astype(jnp.float32)
            level = as_column(lines[0:1] + lines[1:2] + lines[2:3])
            parts.append((level, ref[:rows, at].astype(jnp.float32)))
        top = functools.reduce(jnp.maximum, [level for level, _ in parts])
        shares = [jnp.exp2(level - top) for level, _ in parts]
        total = functools.reduce(jnp.add, shares)
        joined = functools.reduce(jnp.add, [share * part for share, (_, part) in zip(shares, parts)])
        out[:, at] = (gate[:, at] * joined / total).astype(jnp.bfloat16)


def call(kernel, outs, scalars, arrays, flops=0):
    space = [pl.BlockSpec(memory_space=pltpu.SMEM)] * len(scalars) + [pl.BlockSpec(memory_space=pltpu.VMEM)] * len(arrays)
    size = sum(math.prod(a.shape) * a.dtype.itemsize for a in list(arrays) + list(outs))
    return pl.pallas_call(
        kernel,
        out_shape=outs,
        in_specs=space,
        out_specs=[pl.BlockSpec(memory_space=pltpu.VMEM)] * len(outs),
        compiler_params=pltpu.CompilerParams(vmem_limit_bytes=32 * 2**20),
        cost_estimate=pl.CostEstimate(flops=flops, bytes_accessed=size, transcendentals=0),
    )(*scalars, *arrays)


def per_device(q_rows, k_rows, v_rows, q_gain, k_gain, gate_table, clip_lengths, clip_steps):
    rows, width = q_rows.shape
    heads_here = width // HD
    peers = lax.axis_size("head")
    turn = 1 - 2 * (lax.axis_index("dp") % 2)
    place = jnp.stack([lax.axis_index("seq"), lax.axis_size("seq"), turn]).astype(jnp.int32)
    bf16 = functools.partial(jax.ShapeDtypeStruct, dtype=jnp.bfloat16)
    f32 = functools.partial(jax.ShapeDtypeStruct, dtype=jnp.float32)

    v_near, v_next = hop(v_rows, FAR), hop(v_rows, -FAR)
    both = jnp.stack([q_rows, k_rows])
    (squares,) = call(squares_kernel, [f32((peers, 8, rows))], [], [both])
    squares = lax.all_to_all(squares, "head", 0, 0)
    (k_norm,) = call(
        functools.partial(norm_kernel, 1), [bf16((rows, width))], [], [squares, both, k_gain.reshape(1, width)]
    )
    (q_norm,) = call(
        functools.partial(norm_kernel, 0),
        [bf16((rows, width))],
        [],
        [squares, both, q_gain.reshape(1, width), k_norm, v_near],
    )
    k_near, k_next = hop(k_norm, FAR), hop(k_norm, -FAR)
    q_near, q_next = hop(q_norm, 1), hop(q_norm, -1)
    around = [k_near, k_norm, k_next, v_near, v_rows, v_next]
    flops = 4 * rows * 3 * rows * HD * heads_here
    returned = []
    for queries, step in ((q_near, -1), (q_next, 1)):
        (partial,) = call(
            functools.partial(guest_kernel, step),
            [bf16((rows + EXTRA, width))],
            [place, clip_lengths],
            [queries] + around,
            flops,
        )
        returned.append(hop(partial, step))
    from_right, from_left = returned
    mixed, levels, gate = call(
        home_kernel,
        [f32((rows, width))] * 3,
        [place, clip_lengths, clip_steps],
        [gate_table, q_norm] + around,
        flops,
    )
    (out,) = call(
        join_kernel, [bf16((rows, width))], [], [gate, mixed, levels, from_left, from_right]
    )
    return out


def solution(mesh):
    placed = (
        P(("dp", "seq"), "head"),
        P(("dp", "seq"), "head"),
        P(("dp", "seq"), "head"),
        P("head"),
        P("head"),
        P(None, "head"),
        P("dp"),
        P("dp"),
    )
    return jax.shard_map(
        per_device, mesh=mesh, in_specs=placed, out_specs=P(("dp", "seq"), "head"), check_vma=False
    )
```

```python
import functools
import math

import jax
import jax.numpy as jnp
from jax import lax
from jax.experimental import pallas as pl
from jax.experimental.pallas import tpu as pltpu
from jax.sharding import PartitionSpec as P

HEADS = 20
HD = 128
FAR = 3
LOW = -1e30
SCALE2 = HD ** (-0.5) * math.log2(math.e)
EXTRA = 16


def hop(value, steps, by_core=False):
    count, parts = lax.axis_size("seq"), lax.axis_size("dp")
    pairs = []
    for source in range(count):
        for part in range(parts):
            target = source + (-steps if by_core and part % 2 else steps)
            if 0 <= target < count or abs(steps) == 1 or (source, target % count) in ((2, count - 1), (count - FAR, 0)):
                pairs.append((source * parts + part, target % count * parts + part))
    return lax.ppermute(value, ("seq", "dp"), pairs)


def eye(size):
    return lax.broadcasted_iota(jnp.int32, (size, size), 0) == lax.broadcasted_iota(jnp.int32, (size, size), 1)


def as_row(column):
    size = column.shape[0]
    return jnp.sum(jnp.where(eye(size), column, 0.0), axis=0, keepdims=True)


def as_column(row):
    size = row.shape[1]
    return jnp.sum(jnp.where(eye(size), row, 0.0), axis=1, keepdims=True)


def clip_of(positions, lengths_ref):
    end = lengths_ref[0]
    found = (positions >= end).astype(jnp.int32)
    for clip in range(1, lengths_ref.shape[0]):
        end = end + lengths_ref[clip]
        found = found + (positions >= end).astype(jnp.int32)
    return found


def neighbour(place_ref, step):
    block, count = place_ref[0] + step, place_ref[1]
    return jnp.where(block < 0, block + count, jnp.where(block >= count, block - count, block))


def row_clips(block, rows, lengths_ref):
    return clip_of(block * rows + lax.broadcasted_iota(jnp.int32, (rows, 1), 0), lengths_ref)


def key_clips(block, rows, lengths_ref):
    return clip_of(block * rows + lax.broadcasted_iota(jnp.int32, (1, rows), 1), lengths_ref)


def squares_kernel(both_ref, out_ref):
    rows = out_ref.shape[2]
    lines = []
    for index in range(2):
        data = both_ref[index].astype(jnp.float32)
        lines.append(as_row(jnp.sum(data * data, axis=1, keepdims=True)))
    lines = jnp.concatenate(lines + [jnp.zeros((6, rows), jnp.float32)], axis=0)
    for peer in range(out_ref.shape[0]):
        out_ref[peer] = lines


def norm_kernel(index, squares_ref, both_ref, gain_ref, *rest):
    total = squares_ref[0]
    for peer in range(1, squares_ref.shape[0]):
        total = total + squares_ref[peer]
    factors = lax.rsqrt(total / (HEADS * HD) + 1e-06)
    scaled = both_ref[index].astype(jnp.float32) * as_column(factors[index : index + 1])
    rest[-1][...] = (scaled * gain_ref[...]).astype(jnp.bfloat16)


def attend(queries, keys, values, mask):
    heads = range(queries.shape[1] // HD)
    at = [slice(head * HD, (head + 1) * HD) for head in heads]
    scores = [
        lax.dot_general(
            queries[:, at[h]],
            jnp.concatenate([key[:, at[h]] for key in keys], axis=0),
            (((1,), (1,)), ((), ())),
            preferred_element_type=jnp.float32,
        )
        for h in heads
    ]
    scores = [jnp.where(mask, score, LOW) for score in scores]
    highest = [jnp.max(score, axis=1, keepdims=True) for score in scores]
    weights = [jnp.exp2((scores[h] - highest[h]) * SCALE2) for h in heads]
    total = [jnp.sum(weight, axis=1, keepdims=True) for weight in weights]
    mixed = [
        jnp.dot(
            weights[h].astype(jnp.bfloat16),
            jnp.concatenate([value[:, at[h]] for value in values], axis=0),
            preferred_element_type=jnp.float32,
        )
        for h in heads
    ]
    return [(at[h], mixed[h] / total[h], highest[h] * SCALE2 + jnp.log2(total[h])) for h in heads]


def guest_kernel(step, place_ref, lengths_ref, queries, kl, km, kr, vl, vm, vr, out):
    rows, width = queries.shape
    query_ids = row_clips(neighbour(place_ref, step), rows, lengths_ref)
    key_ids = [key_clips(neighbour(place_ref, far * place_ref[2]), rows, lengths_ref) for far in (-FAR, 0, FAR)]
    mask = query_ids == jnp.concatenate(key_ids, axis=1)
    for at, mixed, level in attend(queries, (kl, km, kr), (vl, vm, vr), mask):
        out[:rows, at] = mixed.astype(jnp.bfloat16)
        rest = as_row(level)
        lines = []
        for _ in range(3):
            piece = rest.astype(jnp.bfloat16)
            rest = rest - piece.astype(jnp.float32)
            lines.append(piece.astype(jnp.float32))
        pad = jnp.zeros((EXTRA - 3, rows), jnp.float32)
        out[rows:, at] = jnp.concatenate(lines + [pad], axis=0).astype(jnp.bfloat16)


def home_kernel(place_ref, lengths_ref, steps_ref, table, q, kl, km, kr, vl, vm, vr, mixed_out, level_out, gate_out):
    rows, width = q.shape
    query_ids = row_clips(place_ref[0], rows, lengths_ref)
    key_ids = [key_clips(neighbour(place_ref, far * place_ref[2]), rows, lengths_ref) for far in (-FAR, 0, FAR)]
    mask = query_ids == jnp.concatenate(key_ids, axis=1)
    for at, mixed, level in attend(q, (kl, km, kr), (vl, vm, vr), mask):
        mixed_out[:, at] = mixed
        level_out[:, at] = jnp.broadcast_to(level, (rows, HD))
    gate = jnp.zeros((rows, width), jnp.float32)
    for clip in range(lengths_ref.shape[0]):
        gate = jnp.where(query_ids == clip, table[pl.ds(steps_ref[clip], 1), :], gate)
    gate_out[...] = gate


def join_kernel(gate, mixed, levels, from_left, from_right, out):
    rows, width = mixed.shape
    for head in range(width // HD):
        at = slice(head * HD, (head + 1) * HD)
        parts = [(levels[:, at], mixed[:, at])]
        for ref in (from_left, from_right):
            lines = ref[rows:, at].astype(jnp.float32)
            level = as_column(lines[0:1] + lines[1:2] + lines[2:3])
            parts.append((level, ref[:rows, at].astype(jnp.float32)))
        top = functools.reduce(jnp.maximum, [level for level, _ in parts])
        shares = [jnp.exp2(level - top) for level, _ in parts]
        total = functools.reduce(jnp.add, shares)
        joined = functools.reduce(jnp.add, [share * part for share, (_, part) in zip(shares, parts)])
        out[:, at] = (gate[:, at] * joined / total).astype(jnp.bfloat16)


def call(kernel, outs, scalars, arrays, flops=0):
    space = [pl.BlockSpec(memory_space=pltpu.SMEM)] * len(scalars) + [pl.BlockSpec(memory_space=pltpu.VMEM)] * len(arrays)
    size = sum(math.prod(a.shape) * a.dtype.itemsize for a in list(arrays) + list(outs))
    return pl.pallas_call(
        kernel,
        out_shape=outs,
        in_specs=space,
        out_specs=[pl.BlockSpec(memory_space=pltpu.VMEM)] * len(outs),
        compiler_params=pltpu.CompilerParams(vmem_limit_bytes=32 * 2**20),
        cost_estimate=pl.CostEstimate(flops=flops, bytes_accessed=size, transcendentals=0),
    )(*scalars, *arrays)


def per_device(q_rows, k_rows, v_rows, q_gain, k_gain, gate_table, clip_lengths, clip_steps):
    rows, width = q_rows.shape
    heads_here = width // HD
    peers = lax.axis_size("head")
    turn = 1 - 2 * (lax.axis_index("dp") % 2)
    place = jnp.stack([lax.axis_index("seq"), lax.axis_size("seq"), turn]).astype(jnp.int32)
    bf16 = functools.partial(jax.ShapeDtypeStruct, dtype=jnp.bfloat16)
    f32 = functools.partial(jax.ShapeDtypeStruct, dtype=jnp.float32)

    v_near, v_next = hop(v_rows, FAR, True), hop(v_rows, -FAR, True)
    both = jnp.stack([q_rows, k_rows])
    (squares,) = call(squares_kernel, [f32((peers, 8, rows))], [], [both])
    squares = lax.all_to_all(squares, "head", 0, 0)
    (k_norm,) = call(
        functools.partial(norm_kernel, 1), [bf16((rows, width))], [], [squares, both, k_gain.reshape(1, width)]
    )
    (q_norm,) = call(
        functools.partial(norm_kernel, 0),
        [bf16((rows, width))],
        [],
        [squares, both, q_gain.reshape(1, width), k_norm, v_near],
    )
    k_near, k_next = hop(k_norm, FAR, True), hop(k_norm, -FAR, True)
    q_right, q_left = hop(q_norm, -1), hop(q_norm, 1)
    around = [k_near, k_norm, k_next, v_near, v_rows, v_next]
    flops = 4 * rows * 3 * rows * HD * heads_here
    returned = []
    for queries, step in ((q_right, 1), (q_left, -1)):
        (partial,) = call(
            functools.partial(guest_kernel, step),
            [bf16((rows + EXTRA, width))],
            [place, clip_lengths],
            [queries] + around,
            flops,
        )
        returned.append(hop(partial, step))
    from_left, from_right = returned
    mixed, levels, gate = call(
        home_kernel,
        [f32((rows, width))] * 3,
        [place, clip_lengths, clip_steps],
        [gate_table, q_norm] + around,
        flops,
    )
    (out,) = call(
        join_kernel, [bf16((rows, width))], [], [gate, mixed, levels, from_left, from_right]
    )
    return out


def solution(mesh):
    placed = (
        P(("dp", "seq"), "head"),
        P(("dp", "seq"), "head"),
        P(("dp", "seq"), "head"),
        P("head"),
        P("head"),
        P(None, "head"),
        P("dp"),
        P("dp"),
    )
    return jax.shard_map(
        per_device, mesh=mesh, in_specs=placed, out_specs=P(("dp", "seq"), "head"), check_vma=False
    )
```

```python
import functools
import math

import jax
import jax.numpy as jnp
from jax import lax
from jax.experimental import pallas as pl
from jax.experimental.pallas import tpu as pltpu
from jax.sharding import PartitionSpec as P

HEADS = 20
HD = 128
FAR = 3
LOW = -1e30
SCALE2 = HD ** (-0.5) * math.log2(math.e)
EXTRA = 16


def hop(value, steps, by_core=False):
    count, parts = lax.axis_size("seq"), lax.axis_size("dp")
    pairs = []
    for source in range(count):
        for part in range(parts):
            target = source + (-steps if by_core and part % 2 else steps)
            if 0 <= target < count or abs(steps) == 1 or (source, target % count) in ((2, count - 1), (count - FAR, 0)):
                pairs.append((source * parts + part, target % count * parts + part))
    return lax.ppermute(value, ("seq", "dp"), pairs)


def eye(size):
    return lax.broadcasted_iota(jnp.int32, (size, size), 0) == lax.broadcasted_iota(jnp.int32, (size, size), 1)


def as_row(column):
    size = column.shape[0]
    return jnp.sum(jnp.where(eye(size), column, 0.0), axis=0, keepdims=True)


def as_column(row):
    size = row.shape[1]
    return jnp.sum(jnp.where(eye(size), row, 0.0), axis=1, keepdims=True)


def clip_of(positions, lengths_ref):
    end = lengths_ref[0]
    found = (positions >= end).astype(jnp.int32)
    for clip in range(1, lengths_ref.shape[0]):
        end = end + lengths_ref[clip]
        found = found + (positions >= end).astype(jnp.int32)
    return found


def neighbour(place_ref, step):
    block, count = place_ref[0] + step, place_ref[1]
    return jnp.where(block < 0, block + count, jnp.where(block >= count, block - count, block))


def row_clips(block, rows, lengths_ref):
    return clip_of(block * rows + lax.broadcasted_iota(jnp.int32, (rows, 1), 0), lengths_ref)


def key_clips(block, rows, lengths_ref):
    return clip_of(block * rows + lax.broadcasted_iota(jnp.int32, (1, rows), 1), lengths_ref)


def squares_kernel(q_ref, k_ref, out_ref, held, arrived):
    copies = [
        pltpu.make_async_copy(ref, held.at[index], arrived.at[index]) for index, ref in enumerate((q_ref, k_ref))
    ]
    for copy in copies:
        copy.start()
    rows = out_ref.shape[2]
    lines = []
    for index, copy in enumerate(copies):
        copy.wait()
        data = held[index].astype(jnp.float32)
        lines.append(as_row(jnp.sum(data * data, axis=1, keepdims=True)))
    lines = jnp.concatenate(lines + [jnp.zeros((6, rows), jnp.float32)], axis=0)
    for peer in range(out_ref.shape[0]):
        out_ref[peer] = lines


def norm_kernel(index, squares_ref, data_ref, gain_ref, *rest):
    total = squares_ref[0]
    for peer in range(1, squares_ref.shape[0]):
        total = total + squares_ref[peer]
    factors = lax.rsqrt(total / (HEADS * HD) + 1e-06)
    scaled = data_ref[...].astype(jnp.float32) * as_column(factors[index : index + 1])
    rest[-1][...] = (scaled * gain_ref[...]).astype(jnp.bfloat16)


def attend(queries, keys, values, mask):
    heads = range(queries.shape[1] // HD)
    at = [slice(head * HD, (head + 1) * HD) for head in heads]
    scores = [
        lax.dot_general(
            queries[:, at[h]],
            jnp.concatenate([key[:, at[h]] for key in keys], axis=0),
            (((1,), (1,)), ((), ())),
            preferred_element_type=jnp.float32,
        )
        for h in heads
    ]
    scores = [jnp.where(mask, score, LOW) for score in scores]
    highest = [jnp.max(score, axis=1, keepdims=True) for score in scores]
    weights = [jnp.exp2((scores[h] - highest[h]) * SCALE2) for h in heads]
    total = [jnp.sum(weight, axis=1, keepdims=True) for weight in weights]
    mixed = [
        jnp.dot(
            weights[h].astype(jnp.bfloat16),
            jnp.concatenate([value[:, at[h]] for value in values], axis=0),
            preferred_element_type=jnp.float32,
        )
        for h in heads
    ]
    return [(at[h], mixed[h] / total[h], highest[h] * SCALE2 + jnp.log2(total[h])) for h in heads]


def guest_kernel(step, place_ref, lengths_ref, queries, kl, km, kr, vl, vm, vr, out):
    rows, width = queries.shape
    query_ids = row_clips(neighbour(place_ref, step), rows, lengths_ref)
    key_ids = [key_clips(neighbour(place_ref, far * place_ref[2]), rows, lengths_ref) for far in (-FAR, 0, FAR)]
    mask = query_ids == jnp.concatenate(key_ids, axis=1)
    for at, mixed, level in attend(queries, (kl, km, kr), (vl, vm, vr), mask):
        out[:rows, at] = mixed.astype(jnp.bfloat16)
        rest = as_row(level)
        lines = []
        for _ in range(3):
            piece = rest.astype(jnp.bfloat16)
            rest = rest - piece.astype(jnp.float32)
            lines.append(piece.astype(jnp.float32))
        pad = jnp.zeros((EXTRA - 3, rows), jnp.float32)
        out[rows:, at] = jnp.concatenate(lines + [pad], axis=0).astype(jnp.bfloat16)


def home_kernel(place_ref, lengths_ref, steps_ref, table, q, kl, km, kr, vl, vm, vr, mixed_out, level_out, gate_out):
    rows, width = q.shape
    query_ids = row_clips(place_ref[0], rows, lengths_ref)
    key_ids = [key_clips(neighbour(place_ref, far * place_ref[2]), rows, lengths_ref) for far in (-FAR, 0, FAR)]
    mask = query_ids == jnp.concatenate(key_ids, axis=1)
    for at, mixed, level in attend(q, (kl, km, kr), (vl, vm, vr), mask):
        mixed_out[:, at] = mixed
        level_out[:, at] = jnp.broadcast_to(level, (rows, HD))
    gate = jnp.zeros((rows, width), jnp.float32)
    for clip in range(lengths_ref.shape[0]):
        gate = jnp.where(query_ids == clip, table[pl.ds(steps_ref[clip], 1), :], gate)
    gate_out[...] = gate


def join_kernel(gate, mixed, levels, from_left, from_right, out):
    rows, width = mixed.shape
    for head in range(width // HD):
        at = slice(head * HD, (head + 1) * HD)
        parts = [(levels[:, at], mixed[:, at])]
        for ref in (from_left, from_right):
            lines = ref[rows:, at].astype(jnp.float32)
            level = as_column(lines[0:1] + lines[1:2] + lines[2:3])
            parts.append((level, ref[:rows, at].astype(jnp.float32)))
        top = functools.reduce(jnp.maximum, [level for level, _ in parts])
        shares = [jnp.exp2(level - top) for level, _ in parts]
        total = functools.reduce(jnp.add, shares)
        joined = functools.reduce(jnp.add, [share * part for share, (_, part) in zip(shares, parts)])
        out[:, at] = (gate[:, at] * joined / total).astype(jnp.bfloat16)


def call(kernel, outs, scalars, arrays, flops=0):
    space = [pl.BlockSpec(memory_space=pltpu.SMEM)] * len(scalars) + [pl.BlockSpec(memory_space=pltpu.VMEM)] * len(arrays)
    size = sum(math.prod(a.shape) * a.dtype.itemsize for a in list(arrays) + list(outs))
    return pl.pallas_call(
        kernel,
        out_shape=outs,
        in_specs=space,
        out_specs=[pl.BlockSpec(memory_space=pltpu.VMEM)] * len(outs),
        compiler_params=pltpu.CompilerParams(vmem_limit_bytes=32 * 2**20),
        cost_estimate=pl.CostEstimate(flops=flops, bytes_accessed=size, transcendentals=0),
    )(*scalars, *arrays)


def per_device(q_rows, k_rows, v_rows, q_gain, k_gain, gate_table, clip_lengths, clip_steps):
    rows, width = q_rows.shape
    heads_here = width // HD
    peers = lax.axis_size("head")
    turn = 1 - 2 * (lax.axis_index("dp") % 2)
    place = jnp.stack([lax.axis_index("seq"), lax.axis_size("seq"), turn]).astype(jnp.int32)
    bf16 = functools.partial(jax.ShapeDtypeStruct, dtype=jnp.bfloat16)
    f32 = functools.partial(jax.ShapeDtypeStruct, dtype=jnp.float32)

    v_near, v_next = hop(v_rows, FAR, True), hop(v_rows, -FAR, True)
    squares = pl.pallas_call(
        squares_kernel,
        out_shape=f32((peers, 8, rows)),
        in_specs=[pl.BlockSpec(memory_space=pl.ANY)] * 2,
        out_specs=pl.BlockSpec(memory_space=pltpu.VMEM),
        scratch_shapes=[pltpu.VMEM((2, rows, width), jnp.bfloat16), pltpu.SemaphoreType.DMA((2,))],
    )(q_rows, k_rows)
    squares = lax.all_to_all(squares, "head", 0, 0)
    (k_norm,) = call(
        functools.partial(norm_kernel, 1), [bf16((rows, width))], [], [squares, k_rows, k_gain.reshape(1, width)]
    )
    (q_norm,) = call(
        functools.partial(norm_kernel, 0),
        [bf16((rows, width))],
        [],
        [squares, q_rows, q_gain.reshape(1, width), k_norm, v_near],
    )
    k_near, k_next = hop(k_norm, FAR, True), hop(k_norm, -FAR, True)
    q_right, q_left = hop(q_norm, -1), hop(q_norm, 1)
    around = [k_near, k_norm, k_next, v_near, v_rows, v_next]
    flops = 4 * rows * 3 * rows * HD * heads_here
    returned = []
    for queries, step in ((q_right, 1), (q_left, -1)):
        (partial,) = call(
            functools.partial(guest_kernel, step),
            [bf16((rows + EXTRA, width))],
            [place, clip_lengths],
            [queries] + around,
            flops,
        )
        returned.append(hop(partial, step))
    from_left, from_right = returned
    mixed, levels, gate = call(
        home_kernel,
        [f32((rows, width))] * 3,
        [place, clip_lengths, clip_steps],
        [gate_table, q_norm] + around,
        flops,
    )
    (out,) = call(
        join_kernel, [bf16((rows, width))], [], [gate, mixed, levels, from_left, from_right]
    )
    return out


def solution(mesh):
    placed = (
        P(("dp", "seq"), "head"),
        P(("dp", "seq"), "head"),
        P(("dp", "seq"), "head"),
        P("head"),
        P("head"),
        P(None, "head"),
        P("dp"),
        P("dp"),
    )
    return jax.shard_map(
        per_device, mesh=mesh, in_specs=placed, out_specs=P(("dp", "seq"), "head"), check_vma=False
    )
```
